32 devices in a mesh: occ: 2 (over x), vir: 16 (over z, y, core).
Axes of the slice: x: 2, y: 2, z: 4, core: 2. Of those that a mesh axis runs over, the one named last changes fastest.
Arguments:
- amplitudes: bfloat16 [256, 240, 2112], P(('occ', 'vir')), may hold values from -6 to 6
- integrals: bfloat16 [240, 2112, 256], P('occ', 'vir'), may hold values from -0.01171875 to 0.01171875
- screen: int32 [5, 22], replicated, may hold values 0 or 1
- row_gap: float32 [256], P('occ'), may hold values from 0.2 to 2
- col_gap: float32 [256], P('vir'), may hold values from 0.2 to 2
Outputs:
- update: float32 [256, 256], P('occ', 'vir')
The draws below stay inside these ranges and needn't reach their ends.
Inputs may be any that keep to these rules, and one draw needn't show every extreme that they name: `screen`: 1 keeps the amplitudes of an occupied tile and a virtual tile, 0 screens them out.
All inputs are finite; a program needn't handle non-finite values.
Results may differ from the reference program's by a relative error of at most 0.0003.
Values may be sent and summed in bfloat16 or wider, within the bound.
A program may use at most 128 MiB of HBM per device.

```python
import math
import jax
import jax.numpy as jnp
from jax import lax

O = 240
V = 2112
TILE_O = 48
TILE_V = 96
ROWS = 256
COLS = 256


def set_ends(entries, stream_key, least, largest):
    longest = entries.shape.index(max(entries.shape))
    spots = []
    for shift in (0, 1):
        where = [jax.random.randint(jax.random.fold_in(stream_key, axis), (), 0, length) for axis, length in enumerate(entries.shape)]
        where[longest] = (where[longest] + shift) % entries.shape[longest]
        spots.append(tuple(where))
    return entries.at[spots[0]].set(least).at[spots[1]].set(largest)


def raised(values, own_key, source, target, parts, factor):
    owner, partner = [(jnp.arange(values.shape[axis_at]) // (values.shape[axis_at] // parts)).reshape([-1 if axis == axis_at else 1 for axis in range(values.ndim)]) for axis_at in (source, target)]
    chosen = jax.random.permutation(own_key, parts)[partner]
    strong = (owner == chosen) | (owner == (partner + parts // 2) % parts)
    return jnp.where(strong, factor * values, values)


def levels(stream_key, extent, cuts, least, top_value):
    level, own = 1.0, jax.random.fold_in(stream_key, 6)
    for position, blocks in cuts:
        steps = jnp.exp(jax.random.uniform(jax.random.fold_in(own, position), (blocks,), jnp.float32, least / len(cuts), top_value / len(cuts)))
        level = level * jnp.repeat(steps, extent[position] // blocks).reshape([-1 if axis == position else 1 for axis in range(len(extent))])
    return level


def bell_draw(rng, dims, deviation, bound, pieces=(), kind=jnp.bfloat16):
    array = deviation * jax.random.normal(rng, dims, jnp.float32)
    if pieces:
        array = array * levels(rng, dims, pieces, -0.22, 0.18)
    return jnp.clip(array, -bound, bound).astype(kind)


def gaussian_with(rng, shape, spread, reach, cuts, heavy, held_as=jnp.bfloat16):
    drawn = spread * jax.random.normal(rng, shape, jnp.float32)
    if cuts:
        drawn = drawn * levels(rng, shape, cuts, -0.22, 0.18)
    return jnp.clip(raised(drawn, jax.random.fold_in(rng, 3), *heavy), -reach, reach).astype(held_as)


def setup_inputs(seed: int = 0) -> dict:
    arg_keys = jax.random.split(jax.random.key(seed), 6)
    amplitudes = bell_draw(arg_keys[0], (ROWS, O, V), 1.0, 6.0, ((0, 32),))
    integrals = gaussian_with(arg_keys[1], (O, V, COLS), (O * V) ** -0.5, 0.01171875, ((0, 2), (1, 16)), (1, 2, 16, 2.0))
    screen = set_ends((jax.random.randint(arg_keys[2], (O // TILE_O, V // TILE_V), 0, 3) < 2).astype(jnp.int32), jax.random.fold_in(arg_keys[2], 1), 0, 1)
    row_gap = jnp.clip(jnp.exp(math.log(2.0) - 2.3025851 * jax.random.uniform(arg_keys[3], (ROWS,), jnp.float32) ** levels(arg_keys[3], (ROWS,), ((0, 2),), -0.2, 0.2)), 0.2, 2.0)
    col_gap = jnp.clip(jnp.exp(math.log(2.0) - 2.3025851 * jax.random.uniform(arg_keys[4], (COLS,), jnp.float32) ** levels(arg_keys[4], (COLS,), ((0, 16),), -0.2, 0.2)), 0.2, 2.0)
    return dict(amplitudes=amplitudes, integrals=integrals, screen=screen, row_gap=row_gap, col_gap=col_gap)


def reference(amplitudes, integrals, screen, row_gap, col_gap):
    n_tiles = O // TILE_O

    def add_tile(running, tile_idx):
        offset = tile_idx * TILE_O
        amp_block = lax.dynamic_slice_in_dim(amplitudes, offset, TILE_O, 1).astype(jnp.float32)
        keep_row = lax.dynamic_index_in_dim(screen, tile_idx, 0, keepdims=False)
        keep_mask = jnp.repeat(keep_row, TILE_V).astype(jnp.float32)
        screened = amp_block * keep_mask[None, None, :]
        w_block = lax.dynamic_slice_in_dim(integrals, offset, TILE_O, 0).astype(jnp.float32)
        running = running + jnp.einsum("rkc,kcj->rj", screened, w_block, precision=lax.Precision.HIGHEST)
        return running, None

    zeros_init = jnp.zeros((amplitudes.shape[0], integrals.shape[2]), jnp.float32)
    cycle_sum, unused = lax.scan(add_tile, zeros_init, jnp.arange(n_tiles, dtype=jnp.int32))
    return cycle_sum / (row_gap[:, None] + col_gap[None, :])
```

```python
import functools

import jax
import jax.numpy as jnp
from jax import lax
from jax.experimental import pallas as pl
from jax.experimental.pallas import tpu as pltpu
from jax.sharding import PartitionSpec as P

MESH = pl.DeviceIdType.MESH


def keep_mask(screen, occ_all, vir_all):
    tiles_occ, tiles_vir = screen.shape
    return jnp.broadcast_to(
        screen.astype(jnp.bfloat16)[:, None, :, None],
        (tiles_occ, occ_all // tiles_occ, tiles_vir, vir_all // tiles_vir),
    ).reshape(occ_all, vir_all)


def plain_shards(amplitudes, integrals, screen, row_gap, col_gap):
    occ_all, vir_all = amplitudes.shape[1:]
    screened = amplitudes * keep_mask(screen, occ_all, vir_all)[None]
    occ_part, vir_part, col_total = integrals.shape
    relaid = lax.all_to_all(
        lax.all_to_all(screened[None, None], "occ", split_axis=3, concat_axis=0, tiled=True),
        "vir",
        split_axis=4,
        concat_axis=1,
        tiled=True,
    )
    flat_rows = relaid.reshape(-1, occ_part * vir_part)
    int_slab = integrals.reshape(occ_part * vir_part, col_total)
    per_vir = lax.psum_scatter(
        lax.dot_general(
            int_slab, flat_rows, (((0,), (1,)), ((), ())), preferred_element_type=jnp.float32
        ),
        "vir",
        scatter_dimension=0,
        tiled=True,
    )
    cycle_cols = lax.psum_scatter(per_vir, "occ", scatter_dimension=1, tiled=True)
    return cycle_cols.T / (row_gap[:, None] + col_gap[None, :])


def kernel(
    n_occ, n_vir, group,
    send_ref, int_ref, row_ref, col_ref, out_ref,
    recv, ints, acc, parts, red,
    int_sem, own_sem, send_sems, recv_sems, psend_sems, precv_sems,
):
    n = n_occ * n_vir
    my_occ, my_vir = lax.axis_index("occ"), lax.axis_index("vir")
    me = my_occ * n_vir + my_vir
    vir_part, rows_here = recv.shape[1:3]
    cols_here, rows_out = red.shape[1:]

    load = pltpu.make_async_copy(int_ref, ints, int_sem)
    load.start()

    def target(step):
        to = lax.rem(me + step, n)
        return to // n_vir, lax.rem(to, n_vir)

    barrier = pltpu.get_barrier_semaphore()

    def greet(step, carry):
        pl.semaphore_signal(barrier, inc=1, device_id=target(step), device_id_type=MESH)
        return carry

    lax.fori_loop(1, n, greet, 0)
    pl.semaphore_wait(barrier, n - 1)

    def block(step):
        to_occ, to_vir = target(step)
        return pltpu.make_async_remote_copy(
            src_ref=send_ref.at[to_occ, pl.ds(to_vir * vir_part, vir_part)],
            dst_ref=recv.at[step],
            send_sem=send_sems.at[step],
            recv_sem=recv_sems.at[step],
            device_id=(to_occ, to_vir),
            device_id_type=MESH,
        )

    def send_block(step, carry):
        block(step).start()
        return carry

    lax.fori_loop(1, n, send_block, 0)
    own = pltpu.make_async_copy(
        send_ref.at[my_occ, pl.ds(my_vir * vir_part, vir_part)], recv.at[0], own_sem
    )
    own.start()
    load.wait()
    own.wait()

    for first in range(0, n, group):
        def arrive(step, carry):
            block(step).wait_recv()
            return carry

        lax.fori_loop(max(first, 1), first + group, arrive, 0)

        def multiply(c, total):
            left = recv[first:first + group, c].astype(jnp.float32)
            left = left.reshape(group * rows_here, left.shape[-1]).astype(jnp.bfloat16)
            return total + jnp.dot(left, ints[c], preferred_element_type=jnp.float32)

        total = lax.fori_loop(
            0, vir_part, multiply,
            jnp.zeros((group * rows_here, ints.shape[-1]), jnp.float32),
        )
        for place in range(group):
            origin = lax.rem(me + n - (first + place), n)
            acc[pl.ds(pl.multiple_of(origin * rows_here, rows_here), rows_here), :] = total[
                place * rows_here:(place + 1) * rows_here
            ]

    for half in range(n_occ):
        parts[half] = acc[half * rows_out:(half + 1) * rows_out, :].T

    def piece(step):
        to_occ, to_vir = target(step)
        return pltpu.make_async_remote_copy(
            src_ref=parts.at[
                to_occ, pl.ds(pl.multiple_of(to_vir * cols_here, cols_here), cols_here)
            ],
            dst_ref=red.at[step],
            send_sem=psend_sems.at[step],
            recv_sem=precv_sems.at[step],
            device_id=(to_occ, to_vir),
            device_id_type=MESH,
        )

    def send_piece(step, carry):
        piece(step).start()
        return carry

    lax.fori_loop(1, n, send_piece, 0)

    def add_piece(step, total):
        piece(step).wait_recv()
        return total + red[step]

    mine = parts[my_occ, pl.ds(pl.multiple_of(my_vir * cols_here, cols_here), cols_here), :]
    total = lax.fori_loop(1, n, add_piece, mine)
    out_ref[...] = total / (row_ref[...] + col_ref[...])

    def drain(step, carry):
        block(step).wait_send()
        piece(step).wait_send()
        return carry

    lax.fori_loop(1, n, drain, 0)


def kernel_shards(n_occ, n_vir, amplitudes, integrals, screen, row_gap, col_gap):
    rows_here, occ_all, vir_all = amplitudes.shape
    occ_part, vir_part, col_total = integrals.shape
    n = n_occ * n_vir
    rows_out, cols_here = row_gap.shape[0], col_gap.shape[0]
    screened = amplitudes * keep_mask(screen, occ_all, vir_all)[None]
    send = jnp.transpose(
        screened.reshape(rows_here, n_occ, occ_part, vir_all), (1, 3, 0, 2)
    )
    ints = jnp.transpose(integrals, (1, 0, 2))
    vmem = pl.BlockSpec(memory_space=pltpu.VMEM)
    anywhere = pl.BlockSpec(memory_space=pl.ANY)
    dma = pltpu.SemaphoreType.DMA
    out = pl.pallas_call(
        functools.partial(kernel, n_occ, n_vir, 8),
        out_shape=jax.ShapeDtypeStruct((cols_here, rows_out), jnp.float32),
        in_specs=[anywhere, anywhere, vmem, vmem],
        out_specs=vmem,
        scratch_shapes=[
            pltpu.VMEM((n, vir_part, rows_here, occ_part), jnp.bfloat16),
            pltpu.VMEM((vir_part, occ_part, col_total), jnp.bfloat16),
            pltpu.VMEM((n * rows_here, col_total), jnp.float32),
            pltpu.VMEM((n_occ, col_total, rows_out), jnp.float32),
            pltpu.VMEM((n, cols_here, rows_out), jnp.float32),
            dma, dma, dma((n,)), dma((n,)), dma((n,)), dma((n,)),
        ],
        compiler_params=pltpu.CompilerParams(
            collective_id=0, has_side_effects=True, vmem_limit_bytes=48 * 2**20
        ),
    )(send, ints, row_gap.reshape(1, rows_out), col_gap.reshape(cols_here, 1))
    return out.T


def solution(mesh):
    n_occ, n_vir = mesh.shape["occ"], mesh.shape["vir"]

    def shards(amplitudes, integrals, screen, row_gap, col_gap):
        fits = (
            amplitudes.shape[0] % 8 == 0
            and row_gap.shape[0] % 128 == 0
            and col_gap.shape[0] % 8 == 0
            and (n_occ * n_vir) % 8 == 0
        )
        if fits:
            return kernel_shards(n_occ, n_vir, amplitudes, integrals, screen, row_gap, col_gap)
        return plain_shards(amplitudes, integrals, screen, row_gap, col_gap)

    placed = (P(("occ", "vir"), None, None), P("occ", "vir", None), P(), P("occ"), P("vir"))
    return jax.shard_map(
        shards, mesh=mesh, in_specs=placed, out_specs=P("occ", "vir"), check_vma=False
    )
```

```python
import functools

import jax
import jax.numpy as jnp
from jax import lax
from jax.experimental import pallas as pl
from jax.experimental.pallas import tpu as pltpu
from jax.sharding import PartitionSpec as P

MESH = pl.DeviceIdType.MESH


def keep_mask(screen, occ_all, vir_all):
    tiles_occ, tiles_vir = screen.shape
    return jnp.broadcast_to(
        screen.astype(jnp.bfloat16)[:, None, :, None],
        (tiles_occ, occ_all // tiles_occ, tiles_vir, vir_all // tiles_vir),
    ).reshape(occ_all, vir_all)


def plain_shards(amplitudes, integrals, screen, row_gap, col_gap):
    occ_all, vir_all = amplitudes.shape[1:]
    screened = amplitudes * keep_mask(screen, occ_all, vir_all)[None]
    occ_part, vir_part, col_total = integrals.shape
    relaid = lax.all_to_all(
        lax.all_to_all(screened[None, None], "occ", split_axis=3, concat_axis=0, tiled=True),
        "vir",
        split_axis=4,
        concat_axis=1,
        tiled=True,
    )
    flat_rows = relaid.reshape(-1, occ_part * vir_part)
    int_slab = integrals.reshape(occ_part * vir_part, col_total)
    per_vir = lax.psum_scatter(
        lax.dot_general(
            int_slab, flat_rows, (((0,), (1,)), ((), ())), preferred_element_type=jnp.float32
        ),
        "vir",
        scatter_dimension=0,
        tiled=True,
    )
    cycle_cols = lax.psum_scatter(per_vir, "occ", scatter_dimension=1, tiled=True)
    return cycle_cols.T / (row_gap[:, None] + col_gap[None, :])


def kernel(
    n_occ, n_vir, group,
    send_ref, int_ref, screen_ref, row_ref, col_ref, out_ref,
    recv, ints, acc, parts, red,
    int_sem, own_sem, send_sems, recv_sems, psend_sems, precv_sems,
):
    n = n_occ * n_vir
    my_occ, my_vir = lax.axis_index("occ"), lax.axis_index("vir")
    me = my_occ * n_vir + my_vir
    vir_part, rows_here, occ_part = recv.shape[1:]
    cols_here, rows_out = red.shape[1:]

    tiles_occ, tiles_vir = screen_ref.shape
    tile_occ, tile_vir = occ_part * n_occ // tiles_occ, vir_part * n_vir // tiles_vir
    occ_tile = (
        lax.broadcasted_iota(jnp.int32, (1, occ_part), 1) + my_occ * occ_part
    ) // tile_occ

    def keep(c):
        vir_tile = (my_vir * vir_part + c) // tile_vir
        kept = jnp.zeros((1, occ_part), jnp.float32)
        for t in range(tiles_occ):
            flag = screen_ref[t, vir_tile].astype(jnp.float32)
            kept = jnp.where(occ_tile == t, flag, kept)
        return kept

    load = pltpu.make_async_copy(int_ref, ints, int_sem)
    load.start()

    bits = n.bit_length() - 1
    order = (0, 3, 4, 1, 2) if bits == 5 else tuple(range(bits))

    def partner(step):
        to = me
        for place, bit in enumerate(order):
            flip = lax.rem(step // 2**place, 2)
            to = to + flip * (2**bit - 2 ** (bit + 1) * lax.rem(me // 2**bit, 2))
        return to

    def target(step):
        to = partner(step)
        return to // n_vir, lax.rem(to, n_vir)

    barrier = pltpu.get_barrier_semaphore()

    def greet(step, carry):
        pl.semaphore_signal(barrier, inc=1, device_id=target(step), device_id_type=MESH)
        return carry

    lax.fori_loop(1, n, greet, 0)
    pl.semaphore_wait(barrier, n - 1)

    def block(step):
        to_occ, to_vir = target(step)
        return pltpu.make_async_remote_copy(
            src_ref=send_ref.at[to_occ, pl.ds(to_vir * vir_part, vir_part)],
            dst_ref=recv.at[step],
            send_sem=send_sems.at[step],
            recv_sem=recv_sems.at[step],
            device_id=(to_occ, to_vir),
            device_id_type=MESH,
        )

    def send_block(step, carry):
        block(step).start()
        return carry

    lax.fori_loop(1, n, send_block, 0)
    own = pltpu.make_async_copy(
        send_ref.at[my_occ, pl.ds(my_vir * vir_part, vir_part)], recv.at[0], own_sem
    )
    own.start()
    load.wait()
    own.wait()

    for first in range(0, n, group):
        def arrive(step, carry):
            block(step).wait_recv()
            return carry

        lax.fori_loop(max(first, 1), first + group, arrive, 0)

        def multiply(c, total):
            left = recv[first:first + group, c].astype(jnp.float32)
            left = left.reshape(group * rows_here, occ_part) * keep(c)
            left = left.astype(jnp.bfloat16)
            return total + jnp.dot(left, ints[c], preferred_element_type=jnp.float32)

        total = lax.fori_loop(
            0, vir_part, multiply,
            jnp.zeros((group * rows_here, ints.shape[-1]), jnp.float32),
            unroll=4,
        )
        for place in range(group):
            origin = partner(first + place)
            acc[pl.ds(pl.multiple_of(origin * rows_here, rows_here), rows_here), :] = total[
                place * rows_here:(place + 1) * rows_here
            ]

    for half in range(n_occ):
        parts[half] = acc[half * rows_out:(half + 1) * rows_out, :].T

    def piece(step):
        to_occ, to_vir = target(step)
        return pltpu.make_async_remote_copy(
            src_ref=parts.at[
                to_occ, pl.ds(pl.multiple_of(to_vir * cols_here, cols_here), cols_here)
            ],
            dst_ref=red.at[step],
            send_sem=psend_sems.at[step],
            recv_sem=precv_sems.at[step],
            device_id=(to_occ, to_vir),
            device_id_type=MESH,
        )

    def send_piece(step, carry):
        piece(step).start()
        return carry

    lax.fori_loop(1, n, send_piece, 0)

    def add_piece(step, total):
        piece(step).wait_recv()
        return total + red[step]

    mine = parts[my_occ, pl.ds(pl.multiple_of(my_vir * cols_here, cols_here), cols_here), :]
    total = lax.fori_loop(1, n, add_piece, mine)
    out_ref[...] = total / (row_ref[...] + col_ref[...])

    def drain(step, carry):
        block(step).wait_send()
        piece(step).wait_send()
        return carry

    lax.fori_loop(1, n, drain, 0)


def kernel_shards(n_occ, n_vir, amplitudes, integrals, screen, row_gap, col_gap):
    rows_here, occ_all, vir_all = amplitudes.shape
    occ_part, vir_part, col_total = integrals.shape
    n = n_occ * n_vir
    rows_out, cols_here = row_gap.shape[0], col_gap.shape[0]
    send = jnp.transpose(
        amplitudes.reshape(rows_here, n_occ, occ_part, vir_all), (1, 3, 0, 2)
    )
    ints = jnp.transpose(integrals, (1, 0, 2))
    vmem = pl.BlockSpec(memory_space=pltpu.VMEM)
    anywhere = pl.BlockSpec(memory_space=pl.ANY)
    dma = pltpu.SemaphoreType.DMA
    out = pl.pallas_call(
        functools.partial(kernel, n_occ, n_vir, 8),
        out_shape=jax.ShapeDtypeStruct((cols_here, rows_out), jnp.float32),
        in_specs=[
            anywhere, anywhere, pl.BlockSpec(memory_space=pltpu.SMEM), vmem, vmem
        ],
        out_specs=vmem,
        scratch_shapes=[
            pltpu.VMEM((n, vir_part, rows_here, occ_part), jnp.bfloat16),
            pltpu.VMEM((vir_part, occ_part, col_total), jnp.bfloat16),
            pltpu.VMEM((n * rows_here, col_total), jnp.float32),
            pltpu.VMEM((n_occ, col_total, rows_out), jnp.float32),
            pltpu.VMEM((n, cols_here, rows_out), jnp.float32),
            dma, dma, dma((n,)), dma((n,)), dma((n,)), dma((n,)),
        ],
        compiler_params=pltpu.CompilerParams(
            collective_id=0, has_side_effects=True, vmem_limit_bytes=48 * 2**20
        ),
    )(send, ints, screen, row_gap.reshape(1, rows_out), col_gap.reshape(cols_here, 1))
    return out.T


def solution(mesh):
    n_occ, n_vir = mesh.shape["occ"], mesh.shape["vir"]

    def shards(amplitudes, integrals, screen, row_gap, col_gap):
        fits = (
            amplitudes.shape[0] % 8 == 0
            and row_gap.shape[0] % 128 == 0
            and col_gap.shape[0] % 8 == 0
            and (n_occ * n_vir) % 8 == 0
            and (n_occ * n_vir).bit_count() == 1
        )
        if fits:
            return kernel_shards(n_occ, n_vir, amplitudes, integrals, screen, row_gap, col_gap)
        return plain_shards(amplitudes, integrals, screen, row_gap, col_gap)

    placed = (P(("occ", "vir"), None, None), P("occ", "vir", None), P(), P("occ"), P("vir"))
    return jax.shard_map(
        shards, mesh=mesh, in_specs=placed, out_specs=P("occ", "vir"), check_vma=False
    )
```

```python
import functools

import jax
import jax.numpy as jnp
from jax import lax
from jax.experimental import pallas as pl
from jax.experimental.pallas import tpu as pltpu
from jax.sharding import PartitionSpec as P

MESH = pl.DeviceIdType.MESH


def keep_mask(screen, occ_all, vir_all):
    tiles_occ, tiles_vir = screen.shape
    return jnp.broadcast_to(
        screen.astype(jnp.bfloat16)[:, None, :, None],
        (tiles_occ, occ_all // tiles_occ, tiles_vir, vir_all // tiles_vir),
    ).reshape(occ_all, vir_all)


def plain_shards(amplitudes, integrals, screen, row_gap, col_gap):
    occ_all, vir_all = amplitudes.shape[1:]
    screened = amplitudes * keep_mask(screen, occ_all, vir_all)[None]
    occ_part, vir_part, col_total = integrals.shape
    relaid = lax.all_to_all(
        lax.all_to_all(screened[None, None], "occ", split_axis=3, concat_axis=0, tiled=True),
        "vir",
        split_axis=4,
        concat_axis=1,
        tiled=True,
    )
    flat_rows = relaid.reshape(-1, occ_part * vir_part)
    int_slab = integrals.reshape(occ_part * vir_part, col_total)
    per_vir = lax.psum_scatter(
        lax.dot_general(
            int_slab, flat_rows, (((0,), (1,)), ((), ())), preferred_element_type=jnp.float32
        ),
        "vir",
        scatter_dimension=0,
        tiled=True,
    )
    cycle_cols = lax.psum_scatter(per_vir, "occ", scatter_dimension=1, tiled=True)
    return cycle_cols.T / (row_gap[:, None] + col_gap[None, :])


def kernel(
    n_occ, n_vir, group,
    send_ref, int_ref, screen_ref, row_ref, col_ref, out_ref,
    recv, ints, raw, packed, weights, keeps, acc, parts, red,
    int_sem, raw_sems, send_sems, recv_sems, psend_sems, precv_sems,
):
    n = n_occ * n_vir
    my_occ, my_vir = lax.axis_index("occ"), lax.axis_index("vir")
    me = my_occ * n_vir + my_vir
    vir_part, rows_here, occ_part = raw.shape[1:]
    mains, lanes = recv.shape[1], recv.shape[3]
    extras, spare = vir_part - mains, lanes - occ_part
    cuts = occ_part // spare
    cols_here, rows_out = red.shape[1:]

    tiles_occ, tiles_vir = screen_ref.shape
    tile_occ, tile_vir = occ_part * n_occ // tiles_occ, vir_part * n_vir // tiles_vir
    occ_tile = (
        lax.broadcasted_iota(jnp.int32, (1, occ_part), 1) + my_occ * occ_part
    ) // tile_occ

    def keep(c):
        vir_tile = (my_vir * vir_part + c) // tile_vir
        kept = jnp.zeros((1, occ_part), jnp.float32)
        for t in range(tiles_occ):
            flag = screen_ref[t, vir_tile].astype(jnp.float32)
            kept = jnp.where(occ_tile == t, flag, kept)
        return kept

    load = pltpu.make_async_copy(int_ref, ints, int_sem)
    load.start()
    slots = raw.shape[0]

    bits = n.bit_length() - 1
    order = (0, 3, 4, 1, 2) if bits == 5 else tuple(range(bits))

    def partner(step):
        to = me
        for place, bit in enumerate(order):
            flip = lax.rem(step // 2**place, 2)
            to = to + flip * (2**bit - 2 ** (bit + 1) * lax.rem(me // 2**bit, 2))
        return to

    def target(step):
        to = partner(step)
        return to // n_vir, lax.rem(to, n_vir)

    def fetch(step):
        to_occ, to_vir = target(lax.rem(step, n))
        slot = lax.rem(step, slots)
        return pltpu.make_async_copy(
            send_ref.at[to_occ, pl.ds(to_vir * vir_part, vir_part)],
            raw.at[slot],
            raw_sems.at[slot],
        )

    for step in range(1, slots + 1):
        fetch(step).start()

    barrier = pltpu.get_barrier_semaphore()

    def greet(step, carry):
        pl.semaphore_signal(barrier, inc=1, device_id=target(step), device_id_type=MESH)
        return carry

    lax.fori_loop(1, n, greet, 0)
    pl.semaphore_wait(barrier, n - 1)

    def block(step):
        to_occ, to_vir = target(step)
        return pltpu.make_async_remote_copy(
            src_ref=packed.at[step],
            dst_ref=recv.at[step],
            send_sem=send_sems.at[step],
            recv_sem=recv_sems.at[step],
            device_id=(to_occ, to_vir),
            device_id_type=MESH,
        )

    def pack(slot, dst, place):
        def from_extra(e, carry):
            extra = raw[slot, mains + e].astype(jnp.float32)
            for g in range(cuts):
                t = e * cuts + g
                main = raw[slot, t].astype(jnp.float32)
                piece_here = extra[:, g * spare:(g + 1) * spare]
                dst[place, t] = jnp.concatenate([main, piece_here], 1).astype(jnp.bfloat16)
            return carry

        lax.fori_loop(0, extras, from_extra, 0)
        for t in range(extras * cuts, mains):
            main = raw[slot, t].astype(jnp.float32)
            blank = jnp.zeros((rows_here, spare), jnp.float32)
            dst[place, t] = jnp.concatenate([main, blank], 1).astype(jnp.bfloat16)

    def send_block(step, carry):
        slot = lax.rem(step, slots)
        fetch(step).wait()
        pack(slot, packed, step)
        block(step).start()

        @pl.when(step + slots < n)
        def _():
            fetch(step + slots).start()

        return carry

    lax.fori_loop(1, n, send_block, 0)
    fetch(n).start()
    fetch(n).wait()
    pack(n % slots, recv, 0)
    load.wait()

    def weigh(e, carry):
        extra = ints[mains + e].astype(jnp.float32)
        extra_keep = keep(mains + e)
        for g in range(cuts):
            t = e * cuts + g
            part = slice(g * spare, (g + 1) * spare)
            main = ints[t].astype(jnp.float32)
            weights[t] = jnp.concatenate([main, extra[part]], 0).astype(jnp.bfloat16)
            keeps[t] = jnp.concatenate([keep(t), extra_keep[:, part]], 1)
        return carry

    lax.fori_loop(0, extras, weigh, 0)
    for t in range(extras * cuts, mains):
        main = ints[t].astype(jnp.float32)
        blank = jnp.zeros((spare, main.shape[1]), jnp.float32)
        weights[t] = jnp.concatenate([main, blank], 0).astype(jnp.bfloat16)
        keeps[t] = jnp.concatenate([keep(t), jnp.zeros((1, spare), jnp.float32)], 1)

    for first in range(0, n, group):
        def arrive(step, carry):
            block(step).wait_recv()
            return carry

        lax.fori_loop(max(first, 1), first + group, arrive, 0)

        def multiply(c, total):
            left = recv[first:first + group, c].astype(jnp.float32)
            left = left.reshape(group * rows_here, lanes) * keeps[c]
            left = left.astype(jnp.bfloat16)
            return total + jnp.dot(left, weights[c], preferred_element_type=jnp.float32)

        total = lax.fori_loop(
            0, mains, multiply,
            jnp.zeros((group * rows_here, ints.shape[-1]), jnp.float32),
            unroll=4,
        )
        for place in range(group):
            origin = partner(first + place)
            acc[pl.ds(pl.multiple_of(origin * rows_here, rows_here), rows_here), :] = total[
                place * rows_here:(place + 1) * rows_here
            ]

    for half in range(n_occ):
        parts[half] = acc[half * rows_out:(half + 1) * rows_out, :].T

    def piece(step):
        to_occ, to_vir = target(step)
        return pltpu.make_async_remote_copy(
            src_ref=parts.at[
                to_occ, pl.ds(pl.multiple_of(to_vir * cols_here, cols_here), cols_here)
            ],
            dst_ref=red.at[step],
            send_sem=psend_sems.at[step],
            recv_sem=precv_sems.at[step],
            device_id=(to_occ, to_vir),
            device_id_type=MESH,
        )

    def send_piece(step, carry):
        piece(step).start()
        return carry

    lax.fori_loop(1, n, send_piece, 0)

    def add_piece(step, total):
        piece(step).wait_recv()
        return total + red[step]

    mine = parts[my_occ, pl.ds(pl.multiple_of(my_vir * cols_here, cols_here), cols_here), :]
    total = lax.fori_loop(1, n, add_piece, mine)
    out_ref[...] = total / (row_ref[...] + col_ref[...])

    def drain(step, carry):
        block(step).wait_send()
        piece(step).wait_send()
        return carry

    lax.fori_loop(1, n, drain, 0)


def kernel_shards(n_occ, n_vir, amplitudes, integrals, screen, row_gap, col_gap):
    rows_here, occ_all, vir_all = amplitudes.shape
    occ_part, vir_part, col_total = integrals.shape
    n = n_occ * n_vir
    lanes = 128
    mains = vir_part - vir_part // (occ_part // (lanes - occ_part) + 1)
    rows_out, cols_here = row_gap.shape[0], col_gap.shape[0]
    send = jnp.transpose(
        amplitudes.reshape(rows_here, n_occ, occ_part, vir_all), (1, 3, 0, 2)
    )
    ints = jnp.transpose(integrals, (1, 0, 2))
    vmem = pl.BlockSpec(memory_space=pltpu.VMEM)
    anywhere = pl.BlockSpec(memory_space=pl.ANY)
    dma = pltpu.SemaphoreType.DMA
    out = pl.pallas_call(
        functools.partial(kernel, n_occ, n_vir, 8),
        out_shape=jax.ShapeDtypeStruct((cols_here, rows_out), jnp.float32),
        in_specs=[
            anywhere, anywhere, pl.BlockSpec(memory_space=pltpu.SMEM), vmem, vmem
        ],
        out_specs=vmem,
        scratch_shapes=[
            pltpu.VMEM((n, mains, rows_here, lanes), jnp.bfloat16),
            pltpu.VMEM((vir_part, occ_part, col_total), jnp.bfloat16),
            pltpu.VMEM((4, vir_part, rows_here, occ_part), jnp.bfloat16),
            pltpu.VMEM((n, mains, rows_here, lanes), jnp.bfloat16),
            pltpu.VMEM((mains, lanes, col_total), jnp.bfloat16),
            pltpu.VMEM((mains, 1, lanes), jnp.float32),
            pltpu.VMEM((n * rows_here, col_total), jnp.float32),
            pltpu.VMEM((n_occ, col_total, rows_out), jnp.float32),
            pltpu.VMEM((n, cols_here, rows_out), jnp.float32),
            dma, dma((4,)), dma((n,)), dma((n,)), dma((n,)), dma((n,)),
        ],
        compiler_params=pltpu.CompilerParams(
            collective_id=0, has_side_effects=True, vmem_limit_bytes=57 * 2**20
        ),
    )(send, ints, screen, row_gap.reshape(1, rows_out), col_gap.reshape(cols_here, 1))
    return out.T


def solution(mesh):
    n_occ, n_vir = mesh.shape["occ"], mesh.shape["vir"]

    def shards(amplitudes, integrals, screen, row_gap, col_gap):
        fits = (
            amplitudes.shape[0] % 8 == 0
            and row_gap.shape[0] % 128 == 0
            and col_gap.shape[0] % 8 == 0
            and (n_occ * n_vir) % 8 == 0
            and 64 <= integrals.shape[0] < 128
            and integrals.shape[0] % (128 - integrals.shape[0]) == 0
            and integrals.shape[0] % 8 == 0
            and (n_occ * n_vir).bit_count() == 1
        )
        if fits:
            return kernel_shards(n_occ, n_vir, amplitudes, integrals, screen, row_gap, col_gap)
        return plain_shards(amplitudes, integrals, screen, row_gap, col_gap)

    placed = (P(("occ", "vir"), None, None), P("occ", "vir", None), P(), P("occ"), P("vir"))
    return jax.shard_map(
        shards, mesh=mesh, in_specs=placed, out_specs=P("occ", "vir"), check_vma=False
    )
```

```python
import functools

import jax
import jax.numpy as jnp
from jax import lax
from jax.experimental import pallas as pl
from jax.experimental.pallas import tpu as pltpu
from jax.sharding import PartitionSpec as P

MESH = pl.DeviceIdType.MESH


def keep_mask(screen, occ_all, vir_all):
    tiles_occ, tiles_vir = screen.shape
    return jnp.broadcast_to(
        screen.astype(jnp.bfloat16)[:, None, :, None],
        (tiles_occ, occ_all // tiles_occ, tiles_vir, vir_all // tiles_vir),
    ).reshape(occ_all, vir_all)


def plain_shards(amplitudes, integrals, screen, row_gap, col_gap):
    occ_all, vir_all = amplitudes.shape[1:]
    screened = amplitudes * keep_mask(screen, occ_all, vir_all)[None]
    occ_part, vir_part, col_total = integrals.shape
    relaid = lax.all_to_all(
        lax.all_to_all(screened[None, None], "occ", split_axis=3, concat_axis=0, tiled=True),
        "vir",
        split_axis=4,
        concat_axis=1,
        tiled=True,
    )
    flat_rows = relaid.reshape(-1, occ_part * vir_part)
    int_slab = integrals.reshape(occ_part * vir_part, col_total)
    per_vir = lax.psum_scatter(
        lax.dot_general(
            int_slab, flat_rows, (((0,), (1,)), ((), ())), preferred_element_type=jnp.float32
        ),
        "vir",
        scatter_dimension=0,
        tiled=True,
    )
    cycle_cols = lax.psum_scatter(per_vir, "occ", scatter_dimension=1, tiled=True)
    return cycle_cols.T / (row_gap[:, None] + col_gap[None, :])


def kernel(
    n_occ, n_vir, group,
    send_ref, int_ref, screen_ref, row_ref, col_ref, out_ref,
    recv, ints, raw, packed, weights, keeps, acc, parts, red,
    int_sem, raw_sems, send_sems, recv_sems, psend_sems, precv_sems,
):
    n = n_occ * n_vir
    my_occ, my_vir = lax.axis_index("occ"), lax.axis_index("vir")
    me = my_occ * n_vir + my_vir
    vir_part, rows_here, occ_part = raw.shape[1:]
    mains, lanes = recv.shape[1], recv.shape[3]
    extras, spare = vir_part - mains, lanes - occ_part
    cuts = occ_part // spare
    cols_here, rows_out = red.shape[1:]

    tiles_occ, tiles_vir = screen_ref.shape
    tile_occ, tile_vir = occ_part * n_occ // tiles_occ, vir_part * n_vir // tiles_vir
    occ_tile = (
        lax.broadcasted_iota(jnp.int32, (1, occ_part), 1) + my_occ * occ_part
    ) // tile_occ

    def keep(c):
        vir_tile = (my_vir * vir_part + c) // tile_vir
        kept = jnp.zeros((1, occ_part), jnp.float32)
        for t in range(tiles_occ):
            flag = screen_ref[t, vir_tile].astype(jnp.float32)
            kept = jnp.where(occ_tile == t, flag, kept)
        return kept

    load = pltpu.make_async_copy(int_ref, ints, int_sem)
    load.start()
    slots = raw.shape[0]

    bits = n.bit_length() - 1
    order = (0, 3, 1, 4, 2) if bits == 5 else tuple(range(bits))

    def partner(step):
        to = me
        for place, bit in enumerate(order):
            flip = lax.rem(step // 2**place, 2)
            to = to + flip * (2**bit - 2 ** (bit + 1) * lax.rem(me // 2**bit, 2))
        return to

    def target(step):
        to = partner(step)
        return to // n_vir, lax.rem(to, n_vir)

    def fetch(step):
        to_occ, to_vir = target(lax.rem(step, n))
        slot = lax.rem(step, slots)
        return pltpu.make_async_copy(
            send_ref.at[to_occ, pl.ds(to_vir * vir_part, vir_part)],
            raw.at[slot],
            raw_sems.at[slot],
        )

    for step in range(1, slots + 1):
        fetch(step).start()

    barrier = pltpu.get_barrier_semaphore()

    def greet(step, carry):
        pl.semaphore_signal(barrier, inc=1, device_id=target(step), device_id_type=MESH)
        return carry

    lax.fori_loop(1, n, greet, 0)
    pl.semaphore_wait(barrier, n - 1)

    def block(step):
        to_occ, to_vir = target(step)
        return pltpu.make_async_remote_copy(
            src_ref=packed.at[step],
            dst_ref=recv.at[step],
            send_sem=send_sems.at[step],
            recv_sem=recv_sems.at[step],
            device_id=(to_occ, to_vir),
            device_id_type=MESH,
        )

    def pack(slot, dst, place):
        def from_extra(e, carry):
            extra = raw[slot, mains + e].astype(jnp.float32)
            for g in range(cuts):
                t = e * cuts + g
                main = raw[slot, t].astype(jnp.float32)
                piece_here = extra[:, g * spare:(g + 1) * spare]
                dst[place, t] = jnp.concatenate([main, piece_here], 1).astype(jnp.bfloat16)
            return carry

        lax.fori_loop(0, extras, from_extra, 0)
        for t in range(extras * cuts, mains):
            main = raw[slot, t].astype(jnp.float32)
            blank = jnp.zeros((rows_here, spare), jnp.float32)
            dst[place, t] = jnp.concatenate([main, blank], 1).astype(jnp.bfloat16)

    def send_block(step, carry):
        slot = lax.rem(step, slots)
        fetch(step).wait()
        pack(slot, packed, step)
        block(step).start()

        @pl.when(step + slots < n)
        def _():
            fetch(step + slots).start()

        return carry

    lax.fori_loop(1, n, send_block, 0)
    fetch(n).start()
    fetch(n).wait()
    pack(n % slots, recv, 0)
    load.wait()

    def weigh(e, carry):
        extra = ints[mains + e].astype(jnp.float32)
        extra_keep = keep(mains + e)
        for g in range(cuts):
            t = e * cuts + g
            part = slice(g * spare, (g + 1) * spare)
            main = ints[t].astype(jnp.float32)
            weights[t] = jnp.concatenate([main, extra[part]], 0).astype(jnp.bfloat16)
            keeps[t] = jnp.concatenate([keep(t), extra_keep[:, part]], 1)
        return carry

    lax.fori_loop(0, extras, weigh, 0)
    for t in range(extras * cuts, mains):
        main = ints[t].astype(jnp.float32)
        blank = jnp.zeros((spare, main.shape[1]), jnp.float32)
        weights[t] = jnp.concatenate([main, blank], 0).astype(jnp.bfloat16)
        keeps[t] = jnp.concatenate([keep(t), jnp.zeros((1, spare), jnp.float32)], 1)

    for first in range(0, n, group):
        def arrive(step, carry):
            block(step).wait_recv()
            return carry

        lax.fori_loop(max(first, 1), first + group, arrive, 0)

        def multiply(c, total):
            left = recv[first:first + group, c].astype(jnp.float32)
            left = left.reshape(group * rows_here, lanes) * keeps[c]
            left = left.astype(jnp.bfloat16)
            return total + jnp.dot(left, weights[c], preferred_element_type=jnp.float32)

        total = lax.fori_loop(
            0, mains, multiply,
            jnp.zeros((group * rows_here, ints.shape[-1]), jnp.float32),
            unroll=31,
        )
        for place in range(group):
            origin = partner(first + place)
            acc[pl.ds(pl.multiple_of(origin * rows_here, rows_here), rows_here), :] = total[
                place * rows_here:(place + 1) * rows_here
            ]

    for half in range(n_occ):
        parts[half] = acc[half * rows_out:(half + 1) * rows_out, :].T

    def piece(step):
        to_occ, to_vir = target(step)
        return pltpu.make_async_remote_copy(
            src_ref=parts.at[
                to_occ, pl.ds(pl.multiple_of(to_vir * cols_here, cols_here), cols_here)
            ],
            dst_ref=red.at[step],
            send_sem=psend_sems.at[step],
            recv_sem=precv_sems.at[step],
            device_id=(to_occ, to_vir),
            device_id_type=MESH,
        )

    def send_piece(step, carry):
        piece(step).start()
        return carry

    lax.fori_loop(1, n, send_piece, 0)

    def add_piece(step, total):
        piece(step).wait_recv()
        return total + red[step]

    mine = parts[my_occ, pl.ds(pl.multiple_of(my_vir * cols_here, cols_here), cols_here), :]
    total = lax.fori_loop(1, n, add_piece, mine)
    out_ref[...] = total / (row_ref[...] + col_ref[...])

    def drain(step, carry):
        block(step).wait_send()
        piece(step).wait_send()
        return carry

    lax.fori_loop(1, n, drain, 0)


def kernel_shards(n_occ, n_vir, amplitudes, integrals, screen, row_gap, col_gap):
    rows_here, occ_all, vir_all = amplitudes.shape
    occ_part, vir_part, col_total = integrals.shape
    n = n_occ * n_vir
    lanes = 128
    mains = vir_part - vir_part // (occ_part // (lanes - occ_part) + 1)
    rows_out, cols_here = row_gap.shape[0], col_gap.shape[0]
    send = jnp.transpose(
        amplitudes.reshape(rows_here, n_occ, occ_part, vir_all), (1, 3, 0, 2)
    )
    ints = jnp.transpose(integrals, (1, 0, 2))
    vmem = pl.BlockSpec(memory_space=pltpu.VMEM)
    anywhere = pl.BlockSpec(memory_space=pl.ANY)
    dma = pltpu.SemaphoreType.DMA
    out = pl.pallas_call(
        functools.partial(kernel, n_occ, n_vir, 8),
        out_shape=jax.ShapeDtypeStruct((cols_here, rows_out), jnp.float32),
        in_specs=[
            anywhere, anywhere, pl.BlockSpec(memory_space=pltpu.SMEM), vmem, vmem
        ],
        out_specs=vmem,
        scratch_shapes=[
            pltpu.VMEM((n, mains, rows_here, lanes), jnp.bfloat16),
            pltpu.VMEM((vir_part, occ_part, col_total), jnp.bfloat16),
            pltpu.VMEM((4, vir_part, rows_here, occ_part), jnp.bfloat16),
            pltpu.VMEM((n, mains, rows_here, lanes), jnp.bfloat16),
            pltpu.VMEM((mains, lanes, col_total), jnp.bfloat16),
            pltpu.VMEM((mains, 1, lanes), jnp.float32),
            pltpu.VMEM((n * rows_here, col_total), jnp.float32),
            pltpu.VMEM((n_occ, col_total, rows_out), jnp.float32),
            pltpu.VMEM((n, cols_here, rows_out), jnp.float32),
            dma, dma((4,)), dma((n,)), dma((n,)), dma((n,)), dma((n,)),
        ],
        compiler_params=pltpu.CompilerParams(
            collective_id=0, has_side_effects=True, vmem_limit_bytes=57 * 2**20
        ),
    )(send, ints, screen, row_gap.reshape(1, rows_out), col_gap.reshape(cols_here, 1))
    return out.T


def solution(mesh):
    n_occ, n_vir = mesh.shape["occ"], mesh.shape["vir"]

    def shards(amplitudes, integrals, screen, row_gap, col_gap):
        fits = (
            amplitudes.shape[0] % 8 == 0
            and row_gap.shape[0] % 128 == 0
            and col_gap.shape[0] % 8 == 0
            and (n_occ * n_vir) % 8 == 0
            and 64 <= integrals.shape[0] < 128
            and integrals.shape[0] % (128 - integrals.shape[0]) == 0
            and integrals.shape[0] % 8 == 0
            and (n_occ * n_vir).bit_count() == 1
        )
        if fits:
            return kernel_shards(n_occ, n_vir, amplitudes, integrals, screen, row_gap, col_gap)
        return plain_shards(amplitudes, integrals, screen, row_gap, col_gap)

    placed = (P(("occ", "vir"), None, None), P("occ", "vir", None), P(), P("occ"), P("vir"))
    return jax.shard_map(
        shards, mesh=mesh, in_specs=placed, out_specs=P("occ", "vir"), check_vma=False
    )
```

```python
import functools

import jax
import jax.numpy as jnp
from jax import lax
from jax.experimental import pallas as pl
from jax.experimental.pallas import tpu as pltpu
from jax.sharding import PartitionSpec as P

MESH = pl.DeviceIdType.MESH


def keep_mask(screen, occ_all, vir_all):
    tiles_occ, tiles_vir = screen.shape
    return jnp.broadcast_to(
        screen.astype(jnp.bfloat16)[:, None, :, None],
        (tiles_occ, occ_all // tiles_occ, tiles_vir, vir_all // tiles_vir),
    ).reshape(occ_all, vir_all)


def plain_shards(amplitudes, integrals, screen, row_gap, col_gap):
    occ_all, vir_all = amplitudes.shape[1:]
    screened = amplitudes * keep_mask(screen, occ_all, vir_all)[None]
    occ_part, vir_part, col_total = integrals.shape
    relaid = lax.all_to_all(
        lax.all_to_all(screened[None, None], "occ", split_axis=3, concat_axis=0, tiled=True),
        "vir",
        split_axis=4,
        concat_axis=1,
        tiled=True,
    )
    flat_rows = relaid.reshape(-1, occ_part * vir_part)
    int_slab = integrals.reshape(occ_part * vir_part, col_total)
    per_vir = lax.psum_scatter(
        lax.dot_general(
            int_slab, flat_rows, (((0,), (1,)), ((), ())), preferred_element_type=jnp.float32
        ),
        "vir",
        scatter_dimension=0,
        tiled=True,
    )
    cycle_cols = lax.psum_scatter(per_vir, "occ", scatter_dimension=1, tiled=True)
    return cycle_cols.T / (row_gap[:, None] + col_gap[None, :])


def kernel(
    n_occ, n_vir, group,
    send_ref, int_ref, screen_ref, row_ref, col_ref, out_ref,
    recv, ints, raw, packed, weights, keeps, acc, parts, red,
    int_sem, raw_sems, send_sems, recv_sems, psend_sems, precv_sems,
):
    n = n_occ * n_vir
    my_occ, my_vir = lax.axis_index("occ"), lax.axis_index("vir")
    me = my_occ * n_vir + my_vir
    vir_part, rows_here, occ_part = raw.shape[1:]
    mains, lanes = recv.shape[1], recv.shape[3]
    extras, spare = vir_part - mains, lanes - occ_part
    cuts = occ_part // spare
    cols_here, rows_out = red.shape[1:]

    tiles_occ, tiles_vir = screen_ref.shape
    tile_occ, tile_vir = occ_part * n_occ // tiles_occ, vir_part * n_vir // tiles_vir
    occ_tile = (
        lax.broadcasted_iota(jnp.int32, (1, occ_part), 1) + my_occ * occ_part
    ) // tile_occ

    def keep(c):
        vir_tile = (my_vir * vir_part + c) // tile_vir
        kept = jnp.zeros((1, occ_part), jnp.float32)
        for t in range(tiles_occ):
            flag = screen_ref[t, vir_tile].astype(jnp.float32)
            kept = jnp.where(occ_tile == t, flag, kept)
        return kept

    load = pltpu.make_async_copy(int_ref, ints, int_sem)
    load.start()
    slots = raw.shape[0]

    bits = n.bit_length() - 1
    order = (0, 1, 3, 4, 2) if bits == 5 else tuple(range(bits))

    def partner(step):
        to = me
        for place, bit in enumerate(order):
            flip = lax.rem(step // 2**place, 2)
            to = to + flip * (2**bit - 2 ** (bit + 1) * lax.rem(me // 2**bit, 2))
        return to

    def target(step):
        to = partner(step)
        return to // n_vir, lax.rem(to, n_vir)

    def fetch(step):
        to_occ, to_vir = target(lax.rem(step, n))
        slot = lax.rem(step, slots)
        return pltpu.make_async_copy(
            send_ref.at[to_occ, pl.ds(to_vir * vir_part, vir_part)],
            raw.at[slot],
            raw_sems.at[slot],
        )

    for step in range(1, slots + 1):
        fetch(step).start()

    barrier = pltpu.get_barrier_semaphore()

    def greet(step, carry):
        pl.semaphore_signal(barrier, inc=1, device_id=target(step), device_id_type=MESH)
        return carry

    lax.fori_loop(1, n, greet, 0)
    pl.semaphore_wait(barrier, n - 1)

    def block(step):
        to_occ, to_vir = target(step)
        return pltpu.make_async_remote_copy(
            src_ref=packed.at[step],
            dst_ref=recv.at[step],
            send_sem=send_sems.at[step],
            recv_sem=recv_sems.at[step],
            device_id=(to_occ, to_vir),
            device_id_type=MESH,
        )

    def pack(slot, dst, place):
        def from_extra(e, carry):
            extra = raw[slot, mains + e].astype(jnp.float32)
            for g in range(cuts):
                t = e * cuts + g
                main = raw[slot, t].astype(jnp.float32)
                piece_here = extra[:, g * spare:(g + 1) * spare]
                dst[place, t] = jnp.concatenate([main, piece_here], 1).astype(jnp.bfloat16)
            return carry

        lax.fori_loop(0, extras, from_extra, 0)
        for t in range(extras * cuts, mains):
            main = raw[slot, t].astype(jnp.float32)
            blank = jnp.zeros((rows_here, spare), jnp.float32)
            dst[place, t] = jnp.concatenate([main, blank], 1).astype(jnp.bfloat16)

    def send_block(step, carry):
        slot = lax.rem(step, slots)
        fetch(step).wait()
        pack(slot, packed, step)
        block(step).start()

        @pl.when(step + slots < n)
        def _():
            fetch(step + slots).start()

        return carry

    lax.fori_loop(1, n, send_block, 0)
    fetch(n).start()
    fetch(n).wait()
    pack(n % slots, recv, 0)
    load.wait()

    def weigh(e, carry):
        extra = ints[mains + e].astype(jnp.float32)
        extra_keep = keep(mains + e)
        for g in range(cuts):
            t = e * cuts + g
            part = slice(g * spare, (g + 1) * spare)
            main = ints[t].astype(jnp.float32)
            weights[t] = jnp.concatenate([main, extra[part]], 0).astype(jnp.bfloat16)
            keeps[t] = jnp.concatenate([keep(t), extra_keep[:, part]], 1)
        return carry

    lax.fori_loop(0, extras, weigh, 0)
    for t in range(extras * cuts, mains):
        main = ints[t].astype(jnp.float32)
        blank = jnp.zeros((spare, main.shape[1]), jnp.float32)
        weights[t] = jnp.concatenate([main, blank], 0).astype(jnp.bfloat16)
        keeps[t] = jnp.concatenate([keep(t), jnp.zeros((1, spare), jnp.float32)], 1)

    for first in range(0, n, group):
        def arrive(step, carry):
            block(step).wait_recv()
            return carry

        lax.fori_loop(max(first, 1), first + group, arrive, 0)

        def multiply(c, total):
            left = recv[first:first + group, c].astype(jnp.float32)
            left = left.reshape(group * rows_here, lanes) * keeps[c]
            left = left.astype(jnp.bfloat16)
            return total + jnp.dot(left, weights[c], preferred_element_type=jnp.float32)

        total = lax.fori_loop(
            0, mains, multiply,
            jnp.zeros((group * rows_here, ints.shape[-1]), jnp.float32),
            unroll=31,
        )
        for place in range(group):
            origin = partner(first + place)
            acc[pl.ds(pl.multiple_of(origin * rows_here, rows_here), rows_here), :] = total[
                place * rows_here:(place + 1) * rows_here
            ]

    for half in range(n_occ):
        parts[half] = acc[half * rows_out:(half + 1) * rows_out, :].T

    def piece(step):
        to_occ, to_vir = target(step)
        return pltpu.make_async_remote_copy(
            src_ref=parts.at[
                to_occ, pl.ds(pl.multiple_of(to_vir * cols_here, cols_here), cols_here)
            ],
            dst_ref=red.at[step],
            send_sem=psend_sems.at[step],
            recv_sem=precv_sems.at[step],
            device_id=(to_occ, to_vir),
            device_id_type=MESH,
        )

    def send_piece(step, carry):
        piece(step).start()
        return carry

    lax.fori_loop(1, n, send_piece, 0)

    def add_piece(step, total):
        piece(step).wait_recv()
        return total + red[step]

    mine = parts[my_occ, pl.ds(pl.multiple_of(my_vir * cols_here, cols_here), cols_here), :]
    total = lax.fori_loop(1, n, add_piece, mine)
    out_ref[...] = total / (row_ref[...] + col_ref[...])

    def drain(step, carry):
        block(step).wait_send()
        piece(step).wait_send()
        return carry

    lax.fori_loop(1, n, drain, 0)


def kernel_shards(n_occ, n_vir, amplitudes, integrals, screen, row_gap, col_gap):
    rows_here, occ_all, vir_all = amplitudes.shape
    occ_part, vir_part, col_total = integrals.shape
    n = n_occ * n_vir
    lanes = 128
    mains = vir_part - vir_part // (occ_part // (lanes - occ_part) + 1)
    rows_out, cols_here = row_gap.shape[0], col_gap.shape[0]
    send = jnp.transpose(
        amplitudes.reshape(rows_here, n_occ, occ_part, vir_all), (1, 3, 0, 2)
    )
    ints = jnp.transpose(integrals, (1, 0, 2))
    vmem = pl.BlockSpec(memory_space=pltpu.VMEM)
    anywhere = pl.BlockSpec(memory_space=pl.ANY)
    dma = pltpu.SemaphoreType.DMA
    out = pl.pallas_call(
        functools.partial(kernel, n_occ, n_vir, 8),
        out_shape=jax.ShapeDtypeStruct((cols_here, rows_out), jnp.float32),
        in_specs=[
            anywhere, anywhere, pl.BlockSpec(memory_space=pltpu.SMEM), vmem, vmem
        ],
        out_specs=vmem,
        scratch_shapes=[
            pltpu.VMEM((n, mains, rows_here, lanes), jnp.bfloat16),
            pltpu.VMEM((vir_part, occ_part, col_total), jnp.bfloat16),
            pltpu.VMEM((4, vir_part, rows_here, occ_part), jnp.bfloat16),
            pltpu.VMEM((n, mains, rows_here, lanes), jnp.bfloat16),
            pltpu.VMEM((mains, lanes, col_total), jnp.bfloat16),
            pltpu.VMEM((mains, 1, lanes), jnp.float32),
            pltpu.VMEM((n * rows_here, col_total), jnp.float32),
            pltpu.VMEM((n_occ, col_total, rows_out), jnp.float32),
            pltpu.VMEM((n, cols_here, rows_out), jnp.float32),
            dma, dma((4,)), dma((n,)), dma((n,)), dma((n,)), dma((n,)),
        ],
        compiler_params=pltpu.CompilerParams(
            collective_id=0, has_side_effects=True, vmem_limit_bytes=57 * 2**20
        ),
    )(send, ints, screen, row_gap.reshape(1, rows_out), col_gap.reshape(cols_here, 1))
    return out.T


def solution(mesh):
    n_occ, n_vir = mesh.shape["occ"], mesh.shape["vir"]

    def shards(amplitudes, integrals, screen, row_gap, col_gap):
        fits = (
            amplitudes.shape[0] % 8 == 0
            and row_gap.shape[0] % 128 == 0
            and col_gap.shape[0] % 8 == 0
            and (n_occ * n_vir) % 8 == 0
            and 64 <= integrals.shape[0] < 128
            and integrals.shape[0] % (128 - integrals.shape[0]) == 0
            and integrals.shape[0] % 8 == 0
            and (n_occ * n_vir).bit_count() == 1
        )
        if fits:
            return kernel_shards(n_occ, n_vir, amplitudes, integrals, screen, row_gap, col_gap)
        return plain_shards(amplitudes, integrals, screen, row_gap, col_gap)

    placed = (P(("occ", "vir"), None, None), P("occ", "vir", None), P(), P("occ"), P("vir"))
    return jax.shard_map(
        shards, mesh=mesh, in_specs=placed, out_specs=P("occ", "vir"), check_vma=False
    )
```
